512 devices in a mesh: tm: 32 (over z, y_lo, core), freq: 16 (over x, y_hi).
Axes of the slice: x: 4, y: 8 (y_hi: 4, y_lo: 2; y = y_hi * 2 + y_lo), z: 8, core: 2. Of those that a mesh axis runs over, the one named last changes fastest.
Arguments:
- jones_gains: bfloat16 [1024, 256, 8, 128], P('tm', 'freq'), may hold values from -6 to 6
- right_terms: bfloat16 [1024, 256, 8, 128], P('tm', 'freq'), may hold values from -6 to 6
- normal_diagonal: bfloat16 [1024, 256, 2, 128], P('tm', 'freq'), may hold values from 0.5 to 2
- normal_cross: bfloat16 [1024, 256, 2, 128], P('tm', 'freq'), may hold values from -0.5 to 0.5
- station_flags: int32 [1024, 256, 64], P('tm', 'freq'), may hold values 0 or 1
- time_weights: bfloat16 [1024, 1024], P('tm'), may hold values from -1 to 2
- time_kernel: bfloat16 [1024, 1024], P('tm'), may hold values from -1 to 2
- channel_weights: bfloat16 [256, 256], P('freq'), may hold values from -1 to 2
- channel_kernel: bfloat16 [256, 256], P('freq'), may hold values from -1 to 2
Outputs:
- smoothed_gains: float32 [1024, 256, 8, 128], P('tm', 'freq')
The draws below stay inside these ranges and needn't reach their ends.
All inputs are finite; a program needn't handle non-finite values. No bound on the sum of `station_flags` on one device may be relied on, other than what follows from the above.
Results may differ from the reference program's by a relative error of at most 0.0054.
Values may be sent and summed in bfloat16 or wider, within the bound.
A program may use at most 64 MiB of HBM per device.

```python
import math
import jax
import jax.numpy as jnp
from jax import lax

STATIONS = 64
DIRS = 2
NT = 1024
NF = 256
COLS = 128


def kernel_matrix(key, size):
    row_index = lax.broadcasted_iota(jnp.float32, (size, size), 0)
    column_index = lax.broadcasted_iota(jnp.float32, (size, size), 1)
    envelope = jnp.exp(-jnp.abs(row_index - column_index) / (0.5 * size))
    noise = jax.random.uniform(key, (size, size), jnp.float32, -1.0, 1.0)
    diagonal = jnp.where(row_index == column_index, 0.6, 0.0)
    return diagonal + noise * envelope * (1.4 / math.sqrt(size))


def draw_time_weights(key, part):
    key = jax.random.fold_in(key, 11)
    matrix = kernel_matrix(key, NT)
    return matrix.astype(jnp.bfloat16)


def draw_time_kernel(key, part):
    key = jax.random.fold_in(key, 23)
    matrix = kernel_matrix(key, NT)
    return matrix.astype(jnp.bfloat16)


def draw_channel_weights(key, part):
    key = jax.random.fold_in(key, 37)
    matrix = kernel_matrix(key, NF)
    return matrix.astype(jnp.bfloat16)


def draw_channel_kernel(key, part):
    key = jax.random.fold_in(key, 41)
    matrix = kernel_matrix(key, NF)
    return matrix.astype(jnp.bfloat16)


def set_ends(drawn, stream_key, smallest, high):
    longest = drawn.shape.index(max(drawn.shape))
    spots = []
    for shift in (0, 1):
        where = [jax.random.randint(jax.random.fold_in(stream_key, axis), (), 0, length) for axis, length in enumerate(drawn.shape)]
        where[longest] = (where[longest] + shift) % drawn.shape[longest]
        spots.append(tuple(where))
    return drawn.at[spots[0]].set(smallest).at[spots[1]].set(high)


def block_levels(stream_key, dims, shards, smallest, largest):
    def one(position, blocks):
        steps = jax.random.uniform(jax.random.fold_in(jax.random.fold_in(stream_key, 6), position), (blocks,), jnp.float32, smallest / len(shards), largest / len(shards))
        return jnp.repeat(jnp.exp(steps), dims[position] // blocks).reshape((-1,) + (1,) * (len(dims) - position - 1))

    gain = one(*shards[0])
    for cut in shards[1:]:
        gain = gain * one(*cut)
    return gain


def normal_values(stream_key, shape, width, limit, split=(), dtype=jnp.bfloat16):
    gain = block_levels(stream_key, shape, split, -0.22, 0.18) if split else 1.0
    drawn = jax.random.normal(stream_key, shape, jnp.float32) * width * gain
    return jnp.minimum(jnp.maximum(drawn, -limit), limit).astype(dtype)


def setup_inputs(seed: int = 0) -> dict:
    splits = jax.random.split(jax.random.key(seed), 10)
    jones_gains = normal_values(splits[0], (NT, NF, 8, COLS), 1.0, 6.0, ((0, 32), (1, 16)))
    right_terms = normal_values(splits[1], (NT, NF, 8, COLS), 1.0, 6.0, ((0, 32), (1, 16)))
    normal_diagonal = jnp.clip(jnp.exp(math.log(2.0) - 1.3862944 * jax.random.uniform(splits[2], (NT, NF, 2, COLS), jnp.float32) ** block_levels(splits[2], (NT, NF, 2, COLS), ((0, 32), (1, 16)), -0.2, 0.2)), 0.5, 2.0).astype(jnp.bfloat16)
    normal_cross = jnp.clip(jax.random.uniform(splits[3], (NT, NF, 2, COLS), jnp.float32, -0.5, 0.5) * block_levels(splits[3], (NT, NF, 2, COLS), ((0, 32), (1, 16)), -0.4, 0.0), -0.5, 0.5).astype(jnp.bfloat16)
    station_flags = set_ends((jax.random.randint(splits[4], (NT, NF, STATIONS), 0, 4) < 1).astype(jnp.int32), jax.random.fold_in(splits[4], 1), 0, 1)
    time_weights = draw_time_weights(jax.random.fold_in(splits[9], 71), 0)
    time_kernel = draw_time_kernel(jax.random.fold_in(splits[9], 71), 0)
    channel_weights = draw_channel_weights(jax.random.fold_in(splits[9], 71), 0)
    channel_kernel = draw_channel_kernel(jax.random.fold_in(splits[9], 71), 0)
    return dict(jones_gains=jones_gains, right_terms=right_terms, normal_diagonal=normal_diagonal, normal_cross=normal_cross, station_flags=station_flags, time_weights=time_weights, time_kernel=time_kernel, channel_weights=channel_weights, channel_kernel=channel_kernel)


def product_terms(right_terms, normal_diagonal, normal_cross):
    upper_left = normal_diagonal[:, :, 0]
    lower_right = normal_diagonal[:, :, 1]
    cross_real = normal_cross[:, :, 0]
    cross_imag = normal_cross[:, :, 1]
    entries = []
    for offset in (0, 4):
        lead_real = right_terms[:, :, offset]
        lead_imag = right_terms[:, :, offset + 1]
        tail_real = right_terms[:, :, offset + 2]
        tail_imag = right_terms[:, :, offset + 3]
        left_real = lead_real * upper_left + tail_real * cross_real + tail_imag * cross_imag
        left_imag = lead_imag * upper_left + tail_imag * cross_real - tail_real * cross_imag
        right_real = lead_real * cross_real - lead_imag * cross_imag + tail_real * lower_right
        right_imag = lead_real * cross_imag + lead_imag * cross_real + tail_imag * lower_right
        entries += [left_real, left_imag, right_real, right_imag]
    return jnp.stack(entries, axis=2)


def updated_gains(jones_gains, right_terms, normal_diagonal, normal_cross, station_flags):
    previous = jones_gains.astype(jnp.float32)
    product = product_terms(right_terms.astype(jnp.float32), normal_diagonal.astype(jnp.float32),
                            normal_cross.astype(jnp.float32))
    flags_wide = jnp.tile(station_flags, (1, 1, DIRS))[:, :, None, :]
    return jnp.where(flags_wide == 1, previous, 0.5 * previous + 0.5 * product).astype(jnp.bfloat16)


def reference(jones_gains, right_terms, normal_diagonal, normal_cross, station_flags,
              time_weights, time_kernel, channel_weights, channel_kernel):
    updated = updated_gains(jones_gains, right_terms, normal_diagonal, normal_cross, station_flags)
    stacked = jnp.moveaxis(updated, 2, 0)

    def smooth_component(component):
        time_major = component.reshape(NT, NF * COLS)
        time_mixed = jnp.dot(time_weights, time_major, preferred_element_type=jnp.float32).astype(jnp.bfloat16)
        time_smooth = jnp.dot(time_kernel, time_mixed, preferred_element_type=jnp.float32).astype(jnp.bfloat16)
        time_smooth = time_smooth.reshape(NT, NF, COLS)
        channel_mixed = jnp.einsum('gf,tfc->tgc', channel_weights.astype(jnp.float32),
                                   time_smooth.astype(jnp.float32)).astype(jnp.bfloat16)
        return jnp.einsum('gf,tfc->tgc', channel_kernel.astype(jnp.float32), channel_mixed.astype(jnp.float32))

    result = lax.map(smooth_component, stacked)
    return jnp.moveaxis(result, 0, 2)
```

```python
import functools

import jax
import jax.numpy as jnp
from jax import lax
from jax.experimental import pallas as pl
from jax.experimental.pallas import tpu as pltpu
from jax.sharding import PartitionSpec as P

MESH = pl.DeviceIdType.MESH
BF16 = jnp.bfloat16
F32 = jnp.float32
SX, SY, SZ = 4, 8, 8
CHIPS = SX * SY * SZ
NT_DIMS = (((1,), (1,)), ((), ()))


def place():
    tm, freq = lax.axis_index("tm"), lax.axis_index("freq")
    return freq // 4, (freq % 4) * 2 + (tm // 2) % 2, tm // 4, tm % 2


def device(x, y, z, core):
    return (z * 4 + (y % 2) * 2 + core, x * 4 + y // 2)


def chip_slot(x, y, z):
    return (x * SY + y) * SZ + z


def exchange_kernel(
    jones, right, diagonal, cross, flags, t_weights, t_kernel, f_weights, f_kernel,
    out,
    jones32, right32, diagonal32, cross32, flags_wide, halves, wide32, packed,
    arrived, columns, time_mats, mixed, smooth, freq_own, freq_mats, outgoing,
    returned, parts,
    ready_y, ready_x, half_send, half_recv, tile_send, tile_recv, own_sem,
    mat_send, mat_recv, row_send, row_recv, pair_send, pair_recv,
    freq_send, freq_recv, fpair_send, fpair_recv, back_send, back_recv,
    last_send, last_recv,
):
    x, y, z, core = place()
    low, j = y % 2, x * 4 + y // 2
    sibling = device(x, y, z, 1 - core)

    def on_x(k):
        return device((x + k) % SX, y, z, core)

    def on_y(k):
        return device(x, (y + k) % SY, z, core)

    def on_z(k):
        return device(x, y, (z + k) % SZ, core)

    def signal(semaphore, target):
        pl.semaphore_signal(semaphore, inc=1, device_id=target, device_id_type=MESH)

    def remote(src, dst, send, recv, target):
        pltpu.make_async_remote_copy(
            src_ref=src, dst_ref=dst, send_sem=send, recv_sem=recv,
            device_id=target, device_id_type=MESH,
        ).start()

    def drain(ref, semaphore):
        pltpu.make_async_copy(ref, ref, semaphore).wait()

    barrier = pltpu.get_barrier_semaphore()
    signal(barrier, sibling)
    for k in range(1, SZ):
        signal(barrier, on_z(k))
    for k in range(1, SY):
        signal(barrier, on_y(k))
    for k in range(1, SX):
        signal(barrier, on_x(k))

    rows = 512

    def widen(step, _):
        at = pl.ds(pl.multiple_of(step * rows, rows), rows)
        jones32[at, :] = jones[at, :].astype(F32)
        right32[at, :] = right[at, :].astype(F32)
        return 0

    lax.fori_loop(0, 8, widen, 0)
    diagonal32[...] = diagonal[...].astype(F32)
    cross32[...] = cross[...].astype(F32)
    flagged = flags[...]
    flags_wide[...] = jnp.concatenate([flagged, flagged], axis=1)
    freq_own[0] = f_weights[...]
    freq_own[1] = f_kernel[...]

    def update(f, _):
        def part(ref, k, per):
            return ref[pl.ds(f * per + k, 32, stride=16 * per), :]

        keep = part(flags_wide, 0, 1) == 1
        upper, lower = part(diagonal32, 0, 2), part(diagonal32, 1, 2)
        real, imag = part(cross32, 0, 2), part(cross32, 1, 2)
        for offset in (0, 4):
            lead_r, lead_i, tail_r, tail_i = (part(right32, offset + k, 8) for k in range(4))
            entries = (
                lead_r * upper + tail_r * real + tail_i * imag,
                lead_i * upper + tail_i * real - tail_r * imag,
                lead_r * real - lead_i * imag + tail_r * lower,
                lead_r * imag + lead_i * real + tail_i * lower,
            )
            for k, entry in enumerate(entries):
                previous = part(jones32, offset + k, 8)
                value = jnp.where(keep, previous, 0.5 * previous + 0.5 * entry)
                halves[offset + k, f, core] = value.astype(BF16)
        return 0

    lax.fori_loop(0, 16, update, 0)

    pl.semaphore_wait(barrier, 1 + (SZ - 1) + (SY - 1) + (SX - 1))
    for k in range(1, SY):
        signal(ready_y, on_y(k))
    mine, other = pl.ds(core * 4, 4), pl.ds((1 - core) * 4, 4)
    remote(halves.at[other, :, core], halves.at[other, :, core], half_send, half_recv, sibling)
    pl.semaphore_wait(ready_y, SY - 1)
    for k in range(1, SX):
        signal(ready_x, on_x(k))

    quarter = pl.ds(pl.multiple_of(x * 256, 256), 256)
    block = z * 2 + low
    for m, source in enumerate((t_weights, t_kernel)):
        pltpu.make_async_copy(
            source.at[:, quarter], time_mats.at[m, block, core, :, quarter], own_sem.at[m]
        ).start()

        def send_rows(k, _, m=m, source=source):
            to_z, to_low = (z + k // 2) % SZ, (low + k) % 2
            remote(
                source.at[:, quarter], time_mats.at[m, block, core, :, quarter],
                row_send.at[m], row_recv.at[m],
                device(x, y - low + to_low, to_z, core),
            )
            return 0

        lax.fori_loop(1, 16, send_rows, 0)

    drain(halves.at[other, :, core], half_recv)

    def flip(f, _):
        for pair in range(2):
            stacked = jnp.concatenate(
                [
                    halves[core * 4 + pair * 2 + low, f].reshape(64, 128),
                    halves[core * 4 + pair * 2 + 1 - low, f].reshape(64, 128),
                ],
                axis=0,
            ).astype(F32)
            wide32[pl.ds(pair * 2048 + f, 128, stride=16), :] = stacked.T
        return 0

    lax.fori_loop(0, 16, flip, 0)

    def narrow(step, _):
        at = pl.ds(pl.multiple_of(step * rows, rows), rows)
        packed[at, :] = wide32[at, :].astype(BF16)
        return 0

    lax.fori_loop(0, 8, narrow, 0)

    pl.semaphore_wait(ready_x, SX - 1)
    own_freq = freq_mats.at[core, pl.ds(pl.multiple_of(j * 16, 16), 16)]
    pltpu.make_async_copy(freq_own.at[core], own_freq, own_sem.at[2]).start()

    def send_freq(k, _):
        to_x, to_y = (x + k // 4) % SX, (y + 2 * (k % 4)) % SY
        remote(freq_own.at[core], own_freq, freq_send, freq_recv, device(to_x, to_y, z, core))
        return 0

    lax.fori_loop(1, 16, send_freq, 0)

    def tile(index):
        return pl.ds(pl.multiple_of(index * 16, 16), 16)

    def chip_at(k):
        return (x + k // 64) % SX, (y + (k // 8) % 8) % SY, (z + k % 8) % SZ

    here = block * 16 + j
    me = chip_slot(x, y, z)
    own = pltpu.make_async_copy(packed.at[tile(me)], arrived.at[tile(here)], own_sem.at[3])
    own.start()

    def send_tile(k, _):
        cx, cy, cz = chip_at(k)
        remote(
            packed.at[tile(chip_slot(cx, cy, cz))], arrived.at[tile(here)],
            tile_send, tile_recv, device(cx, cy, cz, core),
        )
        return 0

    lax.fori_loop(1, CHIPS, send_tile, 0)

    for m in range(2):
        pltpu.make_async_copy(
            t_weights.at[:, quarter], time_mats.at[m, block, core, :, quarter], own_sem.at[m]
        ).wait()
        drain(time_mats.at[m, pl.ds(0, 15), core, :, pl.ds(0, 256)], row_recv.at[m])
        for k in range(1, SX):
            remote(
                time_mats.at[m, :, core, :, quarter], time_mats.at[m, :, core, :, quarter],
                mat_send.at[m], mat_recv.at[m], on_x(k),
            )
    pltpu.make_async_copy(freq_own.at[core], own_freq, own_sem.at[2]).wait()
    drain(freq_mats.at[core, pl.ds(0, 240)], freq_recv)
    remote(freq_mats.at[core], freq_mats.at[core], fpair_send, fpair_recv, sibling)
    for m in range(2):
        drain(time_mats.at[m, :, core, :, pl.ds(0, 768)], mat_recv.at[m])
        remote(
            time_mats.at[m, :, core], time_mats.at[m, :, core],
            pair_send.at[m], pair_recv.at[m], sibling,
        )
    drain(freq_mats.at[1 - core], fpair_recv)
    for m in range(2):
        drain(time_mats.at[m, :, 1 - core], pair_recv.at[m])

    own.wait()
    most = pl.ds(0, (CHIPS - 1) * 16)
    drain(arrived.at[most], tile_recv)

    left = lax.broadcasted_iota(jnp.int32, (256, 128), 1) < 64

    def merge(step, _):
        first = arrived[pl.ds(pl.multiple_of(step * 512, 512), 256), :].astype(F32)
        second = arrived[pl.ds(pl.multiple_of(step * 512 + 256, 256), 256), :].astype(F32)
        lanes = pl.ds(pl.multiple_of(step * 128, 128), 128)
        columns[pl.ds(0, 256), lanes] = jnp.where(left, first, second).astype(BF16)
        columns[pl.ds(256, 256), lanes] = pltpu.roll(
            jnp.where(left, second, first), 64, 1
        ).astype(BF16)
        return 0

    lax.fori_loop(0, SZ, merge, 0)

    def apply_time(m, source, target):
        def step(n, _):
            matrix = time_mats[m, pl.ds(n * 4, 4)].reshape(256, 1024)
            lanes = pl.ds(pl.multiple_of(n * 256, 256), 256)
            target[:, lanes] = lax.dot_general(
                source[...], matrix, NT_DIMS, preferred_element_type=F32
            ).astype(BF16)
            return 0

        lax.fori_loop(0, 4, step, 0)

    apply_time(0, columns, mixed)
    apply_time(1, mixed, smooth)

    def channels(n, _):
        lanes = pl.ds(pl.multiple_of(n * 128, 128), 128)
        results = []
        for c in range(2):
            step = jnp.dot(
                freq_mats[0], smooth[pl.ds(c * 256, 256), lanes], preferred_element_type=F32
            ).astype(BF16)
            results.append(jnp.dot(freq_mats[1], step, preferred_element_type=F32))
        turned = pltpu.roll(results[1], 64, 1)
        outgoing[pl.ds(pl.multiple_of(n * 512, 512), 256), :] = jnp.where(
            left, results[0], turned
        ).astype(BF16)
        outgoing[pl.ds(pl.multiple_of(n * 512 + 256, 256), 256), :] = jnp.where(
            left, turned, results[0]
        ).astype(BF16)
        return 0

    lax.fori_loop(0, SZ, channels, 0)

    back = pltpu.make_async_copy(outgoing.at[tile(here)], returned.at[tile(me)], own_sem.at[4])
    back.start()

    def send_back(k, _):
        cx, cy, cz = chip_at(k)
        there = (cz * 2 + cy % 2) * 16 + cx * 4 + cy // 2
        remote(
            outgoing.at[tile(there)], returned.at[tile(me)],
            back_send, back_recv, device(cx, cy, cz, core),
        )
        return 0

    lax.fori_loop(1, CHIPS, send_back, 0)
    back.wait()
    drain(returned.at[most], back_recv)

    def rewiden(step, _):
        at = pl.ds(pl.multiple_of(step * rows, rows), rows)
        right32[at, :] = returned[at, :].astype(F32)
        return 0

    lax.fori_loop(0, 8, rewiden, 0)

    def unflip(f, _):
        for pair in range(2):
            turned = right32[pl.ds(pair * 2048 + f, 128, stride=16), :].T.astype(BF16)
            parts[core * 4 + pair * 2 + low, f] = turned[:64].reshape(2, 32, 128)
            parts[core * 4 + pair * 2 + 1 - low, f] = turned[64:].reshape(2, 32, 128)
        return 0

    lax.fori_loop(0, 16, unflip, 0)

    keep_own = pltpu.make_async_copy(parts.at[mine, :, core], out.at[mine], own_sem.at[5])
    keep_own.start()
    remote(parts.at[mine, :, 1 - core], out.at[mine], last_send, last_recv, sibling)
    keep_own.wait()
    drain(out.at[other], last_recv)

    drain(out.at[mine], last_send)
    drain(halves.at[other, :, core], half_send)
    drain(packed.at[most], tile_send)
    drain(outgoing.at[most], back_send)
    drain(freq_mats.at[core, pl.ds(0, 240)], freq_send)
    drain(freq_mats.at[core], fpair_send)
    for m in range(2):
        drain(time_mats.at[m, pl.ds(0, 15), core, :, pl.ds(0, 256)], row_send.at[m])
        drain(time_mats.at[m, :, core, :, pl.ds(0, 768)], mat_send.at[m])
        drain(time_mats.at[m, :, core], pair_send.at[m])


def place_kernel(parts, out):
    def step(f, _):
        for k in range(8):
            out[pl.ds(f * 8 + k, 32, stride=128), :] = parts[k, f].astype(F32)
        return 0

    lax.fori_loop(0, 16, step, 0)


def body(
    jones_gains, right_terms, normal_diagonal, normal_cross, station_flags,
    time_weights, time_kernel, channel_weights, channel_kernel,
):
    vmem = pl.BlockSpec(memory_space=pltpu.VMEM)
    dma = pltpu.SemaphoreType.DMA
    parts = pl.pallas_call(
        exchange_kernel,
        out_shape=jax.ShapeDtypeStruct((8, 16, 32, 128), BF16),
        in_specs=[vmem] * 9,
        out_specs=vmem,
        scratch_shapes=[
            pltpu.VMEM((4096, 128), F32),
            pltpu.VMEM((4096, 128), F32),
            pltpu.VMEM((1024, 128), F32),
            pltpu.VMEM((1024, 128), F32),
            pltpu.VMEM((512, 128), jnp.int32),
            pltpu.VMEM((8, 16, 2, 32, 128), BF16),
            pltpu.VMEM((4096, 128), F32),
            pltpu.VMEM((4096, 128), BF16),
            pltpu.VMEM((4096, 128), BF16),
            pltpu.VMEM((512, 1024), BF16),
            pltpu.VMEM((2, 16, 2, 32, 1024), BF16),
            pltpu.VMEM((512, 1024), BF16),
            pltpu.VMEM((512, 1024), BF16),
            pltpu.VMEM((2, 16, 256), BF16),
            pltpu.VMEM((2, 256, 256), BF16),
            pltpu.VMEM((4096, 128), BF16),
            pltpu.VMEM((4096, 128), BF16),
            pltpu.VMEM((8, 16, 2, 32, 128), BF16),
            pltpu.SemaphoreType.REGULAR,
            pltpu.SemaphoreType.REGULAR,
            dma, dma, dma, dma,
            dma((6,)),
            dma((2,)), dma((2,)), dma((2,)), dma((2,)), dma((2,)), dma((2,)),
            dma, dma, dma, dma, dma, dma, dma, dma,
        ],
        compiler_params=pltpu.CompilerParams(
            collective_id=0, has_side_effects=True, vmem_limit_bytes=48 * 1024 * 1024
        ),
    )(
        jones_gains.reshape(4096, 128),
        right_terms.reshape(4096, 128),
        normal_diagonal.reshape(1024, 128),
        normal_cross.reshape(1024, 128),
        station_flags.reshape(512, 64),
        time_weights, time_kernel, channel_weights, channel_kernel,
    )
    placed = pl.pallas_call(
        place_kernel,
        out_shape=jax.ShapeDtypeStruct((4096, 128), F32),
        in_specs=[vmem],
        out_specs=vmem,
        compiler_params=pltpu.CompilerParams(vmem_limit_bytes=16 * 1024 * 1024),
    )(parts)
    return placed.reshape(32, 16, 8, 128)


def solution(mesh):
    cells = P("tm", "freq", None, None)
    in_specs = (
        cells, cells, cells, cells, P("tm", "freq", None),
        P("tm", None), P("tm", None), P("freq", None), P("freq", None),
    )
    return jax.shard_map(body, mesh=mesh, in_specs=in_specs, out_specs=cells, check_vma=False)
```

```python
import functools

import jax
import jax.numpy as jnp
from jax import lax
from jax.experimental import pallas as pl
from jax.experimental.pallas import tpu as pltpu
from jax.sharding import PartitionSpec as P

MESH = pl.DeviceIdType.MESH
BF16 = jnp.bfloat16
F32 = jnp.float32
SX, SY, SZ = 4, 8, 8
CHIPS = SX * SY * SZ
MATS = True
CELL, PAIR, FLAG, TILE = 136, 40, 24, 17
NT_DIMS = (((1,), (1,)), ((), ()))


def place():
    tm, freq = lax.axis_index("tm"), lax.axis_index("freq")
    return freq // 4, (freq % 4) * 2 + (tm // 2) % 2, tm // 4, tm % 2


def device(x, y, z, core):
    return (z * 4 + (y % 2) * 2 + core, x * 4 + y // 2)


def chip_slot(x, y, z):
    return (((x % 2) * 2 + x // 2) * SY + y) * SZ + z


def exchange_kernel(
    jones_in, right_in, diagonal_in, cross_in, flags_in, t_weights_in, t_kernel_in,
    f_weights_in, f_kernel_in,
    out,
    jones, right, diagonal, cross, flags, rows_own, freq_own,
    jones32, right32, diagonal32, cross32, flags_wide, halves, wide32, packed,
    arrived, columns, time_mats, mixed, smooth, freq_mats, outgoing,
    returned, parts,
    ready_y, ready_x, load_sem, half_send, half_recv, tile_send, tile_recv, own_sem,
    row_send, row_recv, side_send, side_recv, far_send, far_recv, pair_send, pair_recv,
    freq_send, freq_recv, fpair_send, fpair_recv, back_send, back_recv,
    last_send, last_recv,
):
    x, y, z, core = place()
    low, j = y % 2, x * 4 + y // 2
    block = z * 2 + low
    here = block * 16 + j
    me = chip_slot(x, y, z)
    sibling = device(x, y, z, 1 - core)
    mine, other = pl.ds(core * 4, 4), pl.ds((1 - core) * 4, 4)

    def on_x(k):
        return device((x + k) % SX, y, z, core)

    def on_y(k):
        return device(x, (y + k) % SY, z, core)

    def in_time(k):
        return device(x, y - low + (low + k) % 2, (z + k // 2) % SZ, core)

    def signal(semaphore, target):
        pl.semaphore_signal(semaphore, inc=1, device_id=target, device_id_type=MESH)

    def remote(src, dst, send, recv, target):
        pltpu.make_async_remote_copy(
            src_ref=src, dst_ref=dst, send_sem=send, recv_sem=recv,
            device_id=target, device_id_type=MESH,
        ).start()

    def drain(ref, semaphore):
        pltpu.make_async_copy(ref, ref, semaphore).wait()

    def tile(index):
        return pl.ds(pl.multiple_of(index * 16, 16), 16)

    barrier = pltpu.get_barrier_semaphore()
    signal(barrier, sibling)
    for k in range(1, 16):
        signal(barrier, in_time(k))
    for k in range(1, SY):
        @pl.when((y + k) % SY // 2 != y // 2)
        def _(k=k):
            signal(barrier, on_y(k))
    for k in range(1, SX):
        signal(barrier, on_x(k))

    loads = [
        pltpu.make_async_copy(src, dst, load_sem.at[n])
        for n, (src, dst) in enumerate(
            (
                (t_weights_in, rows_own.at[0]), (t_kernel_in, rows_own.at[1]),
                (f_weights_in, freq_own.at[0]), (f_kernel_in, freq_own.at[1]),
                (right_in, right), (jones_in, jones), (diagonal_in, diagonal),
                (cross_in, cross), (flags_in, flags),
            )
        )
    ]
    for load in loads:
        load.start()
    for load in loads:
        load.wait()

    def spread(t, _):
        def move(src, dst, per, pitch):
            value = src[pl.ds(pl.multiple_of(t * per, per), per), :]
            dst[pl.ds(pl.multiple_of(t * pitch, 8), per), :] = value.astype(dst.dtype)

        move(jones, jones32, 128, CELL)
        move(right, right32, 128, CELL)
        move(diagonal, diagonal32, 32, PAIR)
        move(cross, cross32, 32, PAIR)
        flagged = flags[pl.ds(pl.multiple_of(t * 16, 16), 16), :]
        flags_wide[pl.ds(pl.multiple_of(t * FLAG, 8), 16), :] = jnp.concatenate(
            [flagged, flagged], axis=1
        )
        return 0

    lax.fori_loop(0, 32, spread, 0)

    def update(f, _):
        def part(ref, k, per, pitch):
            return ref[pl.ds(f * per + k, 32, stride=pitch), :]

        keep = part(flags_wide, 0, 1, FLAG) == 1
        upper, lower = part(diagonal32, 0, 2, PAIR), part(diagonal32, 1, 2, PAIR)
        real, imag = part(cross32, 0, 2, PAIR), part(cross32, 1, 2, PAIR)
        for offset in (0, 4):
            lead_r, lead_i, tail_r, tail_i = (
                part(right32, offset + k, 8, CELL) for k in range(4)
            )
            entries = (
                lead_r * upper + tail_r * real + tail_i * imag,
                lead_i * upper + tail_i * real - tail_r * imag,
                lead_r * real - lead_i * imag + tail_r * lower,
                lead_r * imag + lead_i * real + tail_i * lower,
            )
            for k, entry in enumerate(entries):
                previous = part(jones32, offset + k, 8, CELL)
                value = jnp.where(keep, previous, 0.5 * previous + 0.5 * entry)
                halves[offset + k, f, core] = value.astype(BF16)
        return 0

    def update_some(c):
        lax.fori_loop(c * 4, c * 4 + 4, update, 0)

    def send_half(c):
        some = halves.at[other, pl.ds(c * 8, 8), core]
        remote(some, some, half_send.at[c], half_recv.at[c], sibling)

    update_some(0)
    pl.semaphore_wait(barrier, 1 + 15 + (SY - 2) + (SX - 1))
    for k in range(1, SY):
        signal(ready_y, on_y(k))

    quarter = pl.ds(pl.multiple_of(x * 256, 256), 256)

    def own_rows(m):
        return pltpu.make_async_copy(
            rows_own.at[m, :, quarter], time_mats.at[m, block, core, :, quarter], own_sem.at[m]
        )

    for m in range(2 if MATS else 0):
        own_rows(m).start()

        def send_rows(k, _, m=m):
            remote(
                rows_own.at[m, :, quarter], time_mats.at[m, block, core, :, quarter],
                row_send.at[m], row_recv.at[m], in_time(k),
            )
            return 0

        lax.fori_loop(1, 16, send_rows, 0)

    own_channels = freq_mats.at[core, x, y // 2]
    freq_mats[core, x, y // 2] = freq_own[core]
    for k in range(1, SX):
        remote(own_channels, own_channels, freq_send.at[0], freq_recv.at[0], on_x(k))

    update_some(1)
    send_half(0)
    drain(freq_mats.at[core, pl.ds(0, 3), 0], freq_recv.at[0])
    column_channels = freq_mats.at[core, :, y // 2]
    for k in range(2, SY, 2):
        remote(column_channels, column_channels, freq_send.at[1], freq_recv.at[1], on_y(k))
    pl.semaphore_wait(ready_y, SY - 1)
    for k in range(1, SX):
        signal(ready_x, on_x(k))
    update_some(2)
    update_some(3)
    send_half(1)

    def send_sides(m):
        own_rows(m).wait()
        drain(time_mats.at[m, pl.ds(0, 15), core, :, pl.ds(0, 256)], row_recv.at[m])
        ref = time_mats.at[m, :, core, :, quarter]
        remote(ref, ref, side_send.at[m, 0], side_recv.at[m, 0], on_x(1))
        remote(ref, ref, side_send.at[m, 1], side_recv.at[m, 1], on_x(SX - 1))

    def quarter_of(k):
        return pl.ds(pl.multiple_of((x + k) % SX * 256, 256), 256)

    def forward_sides(m):
        ref = time_mats.at[m, pl.ds(0, 8), core, :, quarter_of(SX - 1)]
        drain(time_mats.at[m, :, core, :, quarter_of(SX - 1)], side_recv.at[m, 0])
        remote(ref, ref, far_send.at[m, 0], far_recv.at[m, 0], on_x(1))
        ref = time_mats.at[m, pl.ds(8, 8), core, :, quarter_of(1)]
        drain(time_mats.at[m, :, core, :, quarter_of(1)], side_recv.at[m, 1])
        remote(ref, ref, far_send.at[m, 1], far_recv.at[m, 1], on_x(SX - 1))

    def send_pair(m):
        for side in range(2):
            drain(time_mats.at[m, pl.ds(0, 8), core, :, quarter_of(2)], far_recv.at[m, side])
        ref = time_mats.at[m, :, core]
        remote(ref, ref, pair_send.at[m], pair_recv.at[m], sibling)

    def flip_pair(pair):
        def flip(f, _):
            stacked = jnp.concatenate(
                [
                    halves[core * 4 + pair * 2 + low, f].reshape(64, 128),
                    halves[core * 4 + pair * 2 + 1 - low, f].reshape(64, 128),
                ],
                axis=0,
            )
            wide32[pl.ds(pair * 128 * TILE + f, 128, stride=TILE), :] = stacked.T.astype(F32)
            return 0

        return flip

    def narrow_pair(pair):
        def narrow(step, _):
            for k in range(16):
                index = pair * 128 + step * 16 + k
                packed[tile(index), :] = wide32[pl.ds(index * TILE, 16), :].astype(BF16)
            return 0

        lax.fori_loop(0, 8, narrow, 0)

    def send_tiles(part):
        pair = odd if part < 4 else 1 - odd

        def send_tile(k, _):
            cx = (x // 2 + k // 64) % 2 * 2 + pair
            turn = k // 8 % 8
            cy, cz = (y + turn % 4 * 2 + turn // 4) % SY, (z + k) % SZ
            remote(
                packed.at[tile(chip_slot(cx, cy, cz))], arrived.at[tile(here)],
                tile_send.at[part], tile_recv, device(cx, cy, cz, core),
            )
            return 0

        start = part % 4 * 32
        lax.fori_loop(start + (part == 0), start + 32, send_tile, 0)

    def tiles_sent(part):
        drain(packed.at[pl.ds(0, 496 if part == 0 else 512)], tile_send.at[part])

    odd = x % 2
    for c in range(2):
        drain(halves.at[other, pl.ds(c * 8, 8), core], half_recv.at[c])
        lax.fori_loop(c * 8, c * 8 + 8, flip_pair(odd), 0)
    narrow_pair(odd)
    pl.semaphore_wait(ready_x, SX - 1)
    drain(freq_mats.at[core, :, pl.ds(0, 3)], freq_recv.at[1])
    remote(freq_mats.at[core], freq_mats.at[core], fpair_send, fpair_recv, sibling)
    own = pltpu.make_async_copy(packed.at[tile(me)], arrived.at[tile(here)], own_sem.at[3])
    own.start()
    if MATS:
        send_sides(0)
    send_tiles(0)
    send_tiles(1)
    lax.fori_loop(0, 16, flip_pair(1 - odd), 0)
    narrow_pair(1 - odd)
    if MATS:
        send_sides(1)
    tiles_sent(0)
    send_tiles(2)
    tiles_sent(1)
    send_tiles(3)
    tiles_sent(2)
    send_tiles(4)
    if MATS:
        forward_sides(0)
    tiles_sent(3)
    send_tiles(5)
    if MATS:
        forward_sides(1)
    tiles_sent(4)
    send_tiles(6)
    if MATS:
        send_pair(0)
    tiles_sent(5)
    send_tiles(7)
    if MATS:
        send_pair(1)
    drain(freq_mats.at[1 - core], fpair_recv)

    own.wait()
    most = pl.ds(0, (CHIPS - 1) * 16)
    drain(arrived.at[most], tile_recv)

    left = lax.broadcasted_iota(jnp.int32, (256, 128), 1) < 64

    def merge(step, _):
        first = arrived[pl.ds(pl.multiple_of(step * 512, 512), 256), :].astype(F32)
        second = arrived[pl.ds(pl.multiple_of(step * 512 + 256, 256), 256), :].astype(F32)
        lanes = pl.ds(pl.multiple_of(step * 128, 128), 128)
        columns[pl.ds(0, 256), lanes] = jnp.where(left, first, second).astype(BF16)
        columns[pl.ds(256, 256), lanes] = pltpu.roll(
            jnp.where(left, second, first), 64, 1
        ).astype(BF16)
        return 0

    lax.fori_loop(0, SZ, merge, 0)

    def times(m, source, n):
        matrix = time_mats[m, pl.ds(n * 4, 4)].reshape(256, 1024)
        return lax.dot_general(source[...], matrix, NT_DIMS, preferred_element_type=F32)

    if MATS:
        drain(time_mats.at[0, :, 1 - core], pair_recv.at[0])

    def first_times(n, _):
        mixed[:, pl.ds(pl.multiple_of(n * 256, 256), 256)] = times(0, columns, n).astype(BF16)
        return 0

    lax.fori_loop(0, 4, first_times, 0)

    first_channels, second_channels = (freq_mats[m].reshape(256, 256) for m in range(2))

    def channels(n, _):
        lanes = pl.ds(pl.multiple_of(n % 2 * 512, 512), 512)
        at = pl.ds(pl.multiple_of(n // 2 * 256, 256), 256)
        step = jnp.dot(first_channels, mixed[at, lanes], preferred_element_type=F32).astype(BF16)
        smooth[at, lanes] = jnp.dot(
            second_channels, step, preferred_element_type=F32
        ).astype(BF16)
        return 0

    lax.fori_loop(0, 4, channels, 0)

    back = pltpu.make_async_copy(outgoing.at[tile(here)], returned.at[tile(me)], own_sem.at[4])
    if MATS:
        drain(time_mats.at[1, :, 1 - core], pair_recv.at[1])

    def second_times(step, _):
        ahead = (3 - step) % 4
        pair = ((z + ahead) % SZ, (z + jnp.where(ahead == 0, 4, SZ - ahead)) % SZ)
        matrix = jnp.concatenate(
            [time_mats[1, pl.ds(cz * 2, 2)].reshape(128, 1024) for cz in pair], axis=0
        )
        result = lax.dot_general(smooth[...], matrix, NT_DIMS, preferred_element_type=F32)
        for half, cz in enumerate(pair):
            kept = result[:256, half * 128 : half * 128 + 128]
            turned = pltpu.roll(result[256:, half * 128 : half * 128 + 128], 64, 1)
            outgoing[pl.ds(pl.multiple_of(cz * 512, 512), 256), :] = jnp.where(
                left, kept, turned
            ).astype(BF16)
            outgoing[pl.ds(pl.multiple_of(cz * 512 + 256, 256), 256), :] = jnp.where(
                left, turned, kept
            ).astype(BF16)

        def send_back(k, _):
            cx, cy = (x + k // 16) % SX, (y + k // 2) % SY
            cz = jnp.where(k % 2 == 0, pair[0], pair[1])
            there = (cz * 2 + cy % 2) * 16 + cx * 4 + cy // 2

            @pl.when(there != here)
            def _():
                remote(
                    outgoing.at[tile(there)], returned.at[tile(me)],
                    back_send, back_recv, device(cx, cy, cz, core),
                )

            return 0

        lax.fori_loop(0, 64, send_back, 0)
        return 0

    lax.fori_loop(0, 4, second_times, 0)
    back.start()
    back.wait()
    drain(returned.at[most], back_recv)

    def rewiden(step, _):
        for k in range(16):
            index = step * 16 + k
            wide32[pl.ds(index * TILE, 16), :] = returned[tile(index), :].astype(F32)
        return 0

    lax.fori_loop(0, 16, rewiden, 0)

    def unflip(f, _):
        for pair in range(2):
            turned = wide32[pl.ds(pair * 128 * TILE + f, 128, stride=TILE), :].astype(BF16).T
            parts[core * 4 + pair * 2 + low, f] = turned[:64].reshape(2, 32, 128)
            parts[core * 4 + pair * 2 + 1 - low, f] = turned[64:].reshape(2, 32, 128)
        return 0

    def keep_own(c):
        some = pl.ds(c * 4, 4)
        return pltpu.make_async_copy(
            parts.at[mine, some, core], out.at[mine, some], own_sem.at[5 + c]
        )

    for c in range(4):
        lax.fori_loop(c * 4, c * 4 + 4, unflip, 0)
        keep_own(c).start()
        some = pl.ds(c * 4, 4)
        remote(
            parts.at[mine, some, 1 - core], out.at[mine, some],
            last_send.at[c], last_recv.at[c], sibling,
        )
    for c in range(4):
        keep_own(c).wait()
        drain(out.at[other, pl.ds(c * 4, 4)], last_recv.at[c])

    for c in range(4):
        drain(out.at[mine, pl.ds(c * 4, 4)], last_send.at[c])
    for c in range(2):
        drain(halves.at[other, pl.ds(c * 8, 8), core], half_send.at[c])
    tiles_sent(6)
    tiles_sent(7)
    drain(outgoing.at[most], back_send)
    drain(freq_mats.at[core, pl.ds(0, 3), 0], freq_send.at[0])
    drain(freq_mats.at[core, :, pl.ds(0, 3)], freq_send.at[1])
    drain(freq_mats.at[core], fpair_send)
    for m in range(2 if MATS else 0):
        drain(time_mats.at[m, pl.ds(0, 15), core, :, pl.ds(0, 256)], row_send.at[m])
        for side in range(2):
            drain(time_mats.at[m, :, core, :, pl.ds(0, 256)], side_send.at[m, side])
            drain(time_mats.at[m, pl.ds(0, 8), core, :, pl.ds(0, 256)], far_send.at[m, side])
        drain(time_mats.at[m, :, core], pair_send.at[m])


def place_kernel(parts, out):
    def step(f, _):
        for k in range(8):
            out[pl.ds(f * 8 + k, 16, stride=128), :] = parts[k, f].astype(F32)
        return 0

    lax.fori_loop(0, 16, step, 0)


def body(
    jones_gains, right_terms, normal_diagonal, normal_cross, station_flags,
    time_weights, time_kernel, channel_weights, channel_kernel,
):
    dma = pltpu.SemaphoreType.DMA
    scratch = [
        ((4096, 128), BF16), ((4096, 128), BF16), ((1024, 128), BF16), ((1024, 128), BF16),
        ((512, 64), jnp.int32), ((2, 32, 1024), BF16), ((2, 16, 256), BF16),
        ((32 * CELL, 128), F32), ((32 * CELL, 128), F32),
        ((32 * PAIR, 128), F32), ((32 * PAIR, 128), F32),
        ((32 * FLAG, 128), jnp.int32), ((8, 16, 2, 32, 128), BF16), ((CHIPS * TILE, 128), F32),
        ((4096, 128), BF16), ((4096, 128), BF16), ((512, 1024), BF16),
        ((2, 16, 2, 32, 1024), BF16), ((512, 1024), BF16), ((512, 1024), BF16),
        ((2, 4, 4, 16, 256), BF16), ((4096, 128), BF16), ((4096, 128), BF16),
        ((8, 16, 2, 32, 128), BF16),
    ]
    parts = pl.pallas_call(
        exchange_kernel,
        out_shape=jax.ShapeDtypeStruct((8, 16, 32, 128), BF16),
        in_specs=[pl.BlockSpec(memory_space=pltpu.HBM)] * 9,
        out_specs=pl.BlockSpec(memory_space=pltpu.VMEM),
        scratch_shapes=[
            *(pltpu.VMEM(shape, dtype) for shape, dtype in scratch),
            pltpu.SemaphoreType.REGULAR,
            pltpu.SemaphoreType.REGULAR,
            dma((9,)), dma((2,)), dma((2,)), dma((8,)), dma, dma((9,)),
            dma((2,)), dma((2,)), dma((2, 2)), dma((2, 2)), dma((2, 2)), dma((2, 2)),
            dma((2,)), dma((2,)),
            dma((2,)), dma((2,)), dma, dma, dma, dma, dma((4,)), dma((4,)),
        ],
        compiler_params=pltpu.CompilerParams(
            collective_id=0, has_side_effects=True, vmem_limit_bytes=56 * 1024 * 1024
        ),
    )(
        jones_gains.reshape(4096, 128),
        right_terms.reshape(4096, 128),
        normal_diagonal.reshape(1024, 128),
        normal_cross.reshape(1024, 128),
        station_flags.reshape(512, 64),
        time_weights, time_kernel, channel_weights, channel_kernel,
    )
    placed = pl.pallas_call(
        place_kernel,
        grid=(2,),
        out_shape=jax.ShapeDtypeStruct((4096, 128), F32),
        in_specs=[pl.BlockSpec((8, 16, 16, 128), lambda n: (0, 0, n, 0))],
        out_specs=pl.BlockSpec((2048, 128), lambda n: (n, 0)),
        compiler_params=pltpu.CompilerParams(vmem_limit_bytes=16 * 1024 * 1024),
    )(parts)
    return placed.reshape(32, 16, 8, 128)


def solution(mesh):
    cells = P("tm", "freq", None, None)
    in_specs = (
        cells, cells, cells, cells, P("tm", "freq", None),
        P("tm", None), P("tm", None), P("freq", None), P("freq", None),
    )
    return jax.shard_map(body, mesh=mesh, in_specs=in_specs, out_specs=cells, check_vma=False)
```

```python
import functools

import jax
import jax.numpy as jnp
from jax import lax
from jax.experimental import pallas as pl
from jax.experimental.pallas import tpu as pltpu
from jax.sharding import PartitionSpec as P

MESH = pl.DeviceIdType.MESH
BF16 = jnp.bfloat16
F32 = jnp.float32
SX, SY, SZ = 4, 8, 8
CHIPS = SX * SY * SZ
CELL, PAIR, FLAG, TILE = 136, 40, 24, 17
NT_DIMS = (((1,), (1,)), ((), ()))


def place():
    tm, freq = lax.axis_index("tm"), lax.axis_index("freq")
    return freq // 4, (freq % 4) * 2 + (tm // 2) % 2, tm // 4, tm % 2


def device(x, y, z, core):
    return (z * 4 + (y % 2) * 2 + core, x * 4 + y // 2)


def chip_slot(x, y, z):
    return (((x % 2) * 2 + x // 2) * SY + y) * SZ + z


def exchange_kernel(
    jones_in, right_in, diagonal_in, cross_in, flags_in, t_weights_in, t_kernel_in,
    f_weights_in, f_kernel_in,
    out,
    jones, right, diagonal, cross, flags, rows_own, freq_own,
    jones32, right32, diagonal32, cross32, flags_wide, halves, wide32, packed,
    arrived, columns, time_mats, mixed, smooth, freq_mats, outgoing,
    returned, parts,
    ready_y, ready_x, load_sem, half_send, half_recv, tile_send, tile_recv, own_sem,
    row_send, row_recv, side_send, side_recv, far_send, far_recv, pair_send, pair_recv,
    freq_send, freq_recv, fpair_send, fpair_recv, back_send, back_recv,
    last_send, last_recv,
):
    x, y, z, core = place()
    low, j = y % 2, x * 4 + y // 2
    block = z * 2 + low
    here = block * 16 + j
    me = chip_slot(x, y, z)
    sibling = device(x, y, z, 1 - core)
    mine, other = pl.ds(core * 4, 4), pl.ds((1 - core) * 4, 4)

    def on_x(k):
        return device((x + k) % SX, y, z, core)

    def on_y(k):
        return device(x, (y + k) % SY, z, core)

    def in_time(k):
        return device(x, y - low + (low + k) % 2, (z + k // 2) % SZ, core)

    def signal(semaphore, target):
        pl.semaphore_signal(semaphore, inc=1, device_id=target, device_id_type=MESH)

    def remote(src, dst, send, recv, target):
        pltpu.make_async_remote_copy(
            src_ref=src, dst_ref=dst, send_sem=send, recv_sem=recv,
            device_id=target, device_id_type=MESH,
        ).start()

    def drain(ref, semaphore):
        pltpu.make_async_copy(ref, ref, semaphore).wait()

    def tile(index):
        return pl.ds(pl.multiple_of(index * 16, 16), 16)

    barrier = pltpu.get_barrier_semaphore()
    signal(barrier, sibling)
    for k in range(1, 16):
        signal(barrier, in_time(k))
    for k in range(1, SY):
        @pl.when((y + k) % SY // 2 != y // 2)
        def _(k=k):
            signal(barrier, on_y(k))
    for k in range(1, SX):
        signal(barrier, on_x(k))

    loads = [
        pltpu.make_async_copy(src, dst, load_sem.at[n])
        for n, (src, dst) in enumerate(
            (
                (t_weights_in, rows_own.at[0]), (t_kernel_in, rows_own.at[1]),
                (f_weights_in, freq_own.at[0]), (f_kernel_in, freq_own.at[1]),
                (right_in, right), (jones_in, jones), (diagonal_in, diagonal),
                (cross_in, cross), (flags_in, flags),
            )
        )
    ]
    for load in loads:
        load.start()
    for load in loads:
        load.wait()

    def spread(t, _):
        def move(src, dst, per, pitch):
            value = src[pl.ds(pl.multiple_of(t * per, per), per), :]
            dst[pl.ds(pl.multiple_of(t * pitch, 8), per), :] = value.astype(dst.dtype)

        move(jones, jones32, 128, CELL)
        move(right, right32, 128, CELL)
        move(diagonal, diagonal32, 32, PAIR)
        move(cross, cross32, 32, PAIR)
        flagged = flags[pl.ds(pl.multiple_of(t * 16, 16), 16), :]
        flags_wide[pl.ds(pl.multiple_of(t * FLAG, 8), 16), :] = jnp.concatenate(
            [flagged, flagged], axis=1
        )
        return 0

    lax.fori_loop(0, 32, spread, 0)

    def update(f, _):
        def part(ref, k, per, pitch):
            return ref[pl.ds(f * per + k, 32, stride=pitch), :]

        keep = part(flags_wide, 0, 1, FLAG) == 1
        upper, lower = part(diagonal32, 0, 2, PAIR), part(diagonal32, 1, 2, PAIR)
        real, imag = part(cross32, 0, 2, PAIR), part(cross32, 1, 2, PAIR)
        for offset in (0, 4):
            lead_r, lead_i, tail_r, tail_i = (
                part(right32, offset + k, 8, CELL) for k in range(4)
            )
            entries = (
                lead_r * upper + tail_r * real + tail_i * imag,
                lead_i * upper + tail_i * real - tail_r * imag,
                lead_r * real - lead_i * imag + tail_r * lower,
                lead_r * imag + lead_i * real + tail_i * lower,
            )
            for k, entry in enumerate(entries):
                previous = part(jones32, offset + k, 8, CELL)
                value = jnp.where(keep, previous, 0.5 * previous + 0.5 * entry)
                halves[offset + k, f, core] = value.astype(BF16)
        return 0

    def update_some(c):
        lax.fori_loop(c * 4, c * 4 + 4, update, 0)

    def send_half(c):
        some = halves.at[other, pl.ds(c * 8, 8), core]
        remote(some, some, half_send.at[c], half_recv.at[c], sibling)

    update_some(0)
    pl.semaphore_wait(barrier, 1 + 15 + (SY - 2) + (SX - 1))
    for k in range(1, SY):
        signal(ready_y, on_y(k))

    quarter = pl.ds(pl.multiple_of(x * 256, 256), 256)

    def own_rows(m):
        return pltpu.make_async_copy(
            rows_own.at[m, :, quarter], time_mats.at[m, block, core, :, quarter], own_sem.at[m]
        )

    for m in range(2):
        own_rows(m).start()

        def send_rows(k, _, m=m):
            remote(
                rows_own.at[m, :, quarter], time_mats.at[m, block, core, :, quarter],
                row_send.at[m], row_recv.at[m], in_time(k),
            )
            return 0

        lax.fori_loop(1, 16, send_rows, 0)

    own_channels = freq_mats.at[core, x, y // 2]
    freq_mats[core, x, y // 2] = freq_own[core]
    for k in range(1, SX):
        remote(own_channels, own_channels, freq_send.at[0], freq_recv.at[0], on_x(k))

    update_some(1)
    send_half(0)
    drain(freq_mats.at[core, pl.ds(0, 3), 0], freq_recv.at[0])
    column_channels = freq_mats.at[core, :, y // 2]
    for k in range(2, SY, 2):
        remote(column_channels, column_channels, freq_send.at[1], freq_recv.at[1], on_y(k))
    pl.semaphore_wait(ready_y, SY - 1)
    for k in range(1, SX):
        signal(ready_x, on_x(k))
    update_some(2)
    update_some(3)
    send_half(1)

    def send_sides(m):
        own_rows(m).wait()
        drain(time_mats.at[m, pl.ds(0, 15), core, :, pl.ds(0, 256)], row_recv.at[m])
        ref = time_mats.at[m, :, core, :, quarter]
        remote(ref, ref, side_send.at[m, 0], side_recv.at[m, 0], on_x(1))
        remote(ref, ref, side_send.at[m, 1], side_recv.at[m, 1], on_x(SX - 1))

    def quarter_of(k):
        return pl.ds(pl.multiple_of((x + k) % SX * 256, 256), 256)

    def forward_sides(m):
        ref = time_mats.at[m, pl.ds(0, 8), core, :, quarter_of(SX - 1)]
        drain(time_mats.at[m, :, core, :, quarter_of(SX - 1)], side_recv.at[m, 0])
        remote(ref, ref, far_send.at[m, 0], far_recv.at[m, 0], on_x(1))
        ref = time_mats.at[m, pl.ds(8, 8), core, :, quarter_of(1)]
        drain(time_mats.at[m, :, core, :, quarter_of(1)], side_recv.at[m, 1])
        remote(ref, ref, far_send.at[m, 1], far_recv.at[m, 1], on_x(SX - 1))

    def send_pair(m):
        for side in range(2):
            drain(time_mats.at[m, pl.ds(0, 8), core, :, quarter_of(2)], far_recv.at[m, side])
        ref = time_mats.at[m, :, core]
        remote(ref, ref, pair_send.at[m], pair_recv.at[m], sibling)

    def flip_pair(pair):
        def flip(f, _):
            stacked = jnp.concatenate(
                [
                    halves[core * 4 + pair * 2 + low, f].reshape(64, 128),
                    halves[core * 4 + pair * 2 + 1 - low, f].reshape(64, 128),
                ],
                axis=0,
            )
            wide32[pl.ds(pair * 128 * TILE + f, 128, stride=TILE), :] = stacked.T.astype(F32)
            return 0

        return flip

    def narrow_pair(pair):
        def narrow(step, _):
            for k in range(16):
                index = pair * 128 + step * 16 + k
                packed[tile(index), :] = wide32[pl.ds(index * TILE, 16), :].astype(BF16)
            return 0

        lax.fori_loop(0, 8, narrow, 0)

    def send_tiles(part):
        pair = odd if part < 4 else 1 - odd

        def send_tile(k, _):
            cx = (x // 2 + k // 64) % 2 * 2 + pair
            turn = k // 8 % 8
            cy, cz = (y + turn % 4 * 2 + turn // 4) % SY, (z + k) % SZ
            remote(
                packed.at[tile(chip_slot(cx, cy, cz))], arrived.at[tile(here)],
                tile_send.at[part], tile_recv, device(cx, cy, cz, core),
            )
            return 0

        start = part % 4 * 32
        lax.fori_loop(start + (part == 0), start + 32, send_tile, 0)

    def tiles_sent(part):
        drain(packed.at[pl.ds(0, 496 if part == 0 else 512)], tile_send.at[part])

    odd = x % 2
    for c in range(2):
        drain(halves.at[other, pl.ds(c * 8, 8), core], half_recv.at[c])
        lax.fori_loop(c * 8, c * 8 + 8, flip_pair(odd), 0)
    narrow_pair(odd)
    pl.semaphore_wait(ready_x, SX - 1)
    drain(freq_mats.at[core, :, pl.ds(0, 3)], freq_recv.at[1])
    remote(freq_mats.at[core], freq_mats.at[core], fpair_send, fpair_recv, sibling)
    own = pltpu.make_async_copy(packed.at[tile(me)], arrived.at[tile(here)], own_sem.at[3])
    own.start()
    send_sides(0)
    send_tiles(0)
    send_tiles(1)
    lax.fori_loop(0, 16, flip_pair(1 - odd), 0)
    narrow_pair(1 - odd)
    send_sides(1)
    tiles_sent(0)
    send_tiles(2)
    tiles_sent(1)
    send_tiles(3)
    tiles_sent(2)
    send_tiles(4)
    forward_sides(0)
    tiles_sent(3)
    send_tiles(5)
    forward_sides(1)
    tiles_sent(4)
    send_tiles(6)
    send_pair(0)
    tiles_sent(5)
    send_tiles(7)
    send_pair(1)
    drain(freq_mats.at[1 - core], fpair_recv)

    own.wait()
    most = pl.ds(0, (CHIPS - 1) * 16)
    drain(arrived.at[most], tile_recv)

    left = lax.broadcasted_iota(jnp.int32, (256, 128), 1) < 64

    def merge(step, _):
        first = arrived[pl.ds(pl.multiple_of(step * 512, 512), 256), :].astype(F32)
        second = arrived[pl.ds(pl.multiple_of(step * 512 + 256, 256), 256), :].astype(F32)
        lanes = pl.ds(pl.multiple_of(step * 128, 128), 128)
        columns[pl.ds(0, 256), lanes] = jnp.where(left, first, second).astype(BF16)
        columns[pl.ds(256, 256), lanes] = pltpu.roll(
            jnp.where(left, second, first), 64, 1
        ).astype(BF16)
        return 0

    lax.fori_loop(0, SZ, merge, 0)

    def times(m, source, n):
        matrix = time_mats[m, pl.ds(n * 4, 4)].reshape(256, 1024)
        return lax.dot_general(source[...], matrix, NT_DIMS, preferred_element_type=F32)

    drain(time_mats.at[0, :, 1 - core], pair_recv.at[0])

    for n in range(4):
        mixed[:, n * 256 : n * 256 + 256] = times(0, columns, n).astype(BF16)

    first_channels, second_channels = (freq_mats[m].reshape(256, 256) for m in range(2))

    for c in range(2):
        at = pl.ds(c * 256, 256)
        step = jnp.dot(first_channels, mixed[at, :], preferred_element_type=F32).astype(BF16)
        smooth[at, :] = jnp.dot(
            second_channels, step, preferred_element_type=F32
        ).astype(BF16)

    back = pltpu.make_async_copy(outgoing.at[tile(here)], returned.at[tile(me)], own_sem.at[4])
    drain(time_mats.at[1, :, 1 - core], pair_recv.at[1])

    def second_times(step, _):
        ahead = (3 - step) % 4
        pair = ((z + ahead) % SZ, (z + jnp.where(ahead == 0, 4, SZ - ahead)) % SZ)
        matrix = jnp.concatenate(
            [time_mats[1, pl.ds(cz * 2, 2)].reshape(128, 1024) for cz in pair], axis=0
        )
        result = lax.dot_general(smooth[...], matrix, NT_DIMS, preferred_element_type=F32)
        for half, cz in enumerate(pair):
            kept = result[:256, half * 128 : half * 128 + 128]
            turned = pltpu.roll(result[256:, half * 128 : half * 128 + 128], 64, 1)
            outgoing[pl.ds(pl.multiple_of(cz * 512, 512), 256), :] = jnp.where(
                left, kept, turned
            ).astype(BF16)
            outgoing[pl.ds(pl.multiple_of(cz * 512 + 256, 256), 256), :] = jnp.where(
                left, turned, kept
            ).astype(BF16)

        def send_back(k, _):
            cx, cy = (x + k // 16) % SX, (y + k // 2) % SY
            cz = jnp.where(k % 2 == 0, pair[0], pair[1])
            there = (cz * 2 + cy % 2) * 16 + cx * 4 + cy // 2

            @pl.when(there != here)
            def _():
                remote(
                    outgoing.at[tile(there)], returned.at[tile(me)],
                    back_send, back_recv, device(cx, cy, cz, core),
                )

            return 0

        lax.fori_loop(0, 64, send_back, 0)
        return 0

    lax.fori_loop(0, 4, second_times, 0)
    back.start()
    back.wait()
    drain(returned.at[most], back_recv)

    def rewiden(step, _):
        for k in range(16):
            index = step * 16 + k
            wide32[pl.ds(index * TILE, 16), :] = returned[tile(index), :].astype(F32)
        return 0

    lax.fori_loop(0, 16, rewiden, 0)

    def unflip(f, _):
        for pair in range(2):
            turned = wide32[pl.ds(pair * 128 * TILE + f, 128, stride=TILE), :].astype(BF16).T
            parts[core * 4 + pair * 2 + low, f] = turned[:64].reshape(2, 32, 128)
            parts[core * 4 + pair * 2 + 1 - low, f] = turned[64:].reshape(2, 32, 128)
        return 0

    def keep_own(c):
        some = pl.ds(c * 4, 4)
        return pltpu.make_async_copy(
            parts.at[mine, some, core], out.at[mine, some], own_sem.at[5 + c]
        )

    for c in range(4):
        lax.fori_loop(c * 4, c * 4 + 4, unflip, 0)
        keep_own(c).start()
        some = pl.ds(c * 4, 4)
        remote(
            parts.at[mine, some, 1 - core], out.at[mine, some],
            last_send.at[c], last_recv.at[c], sibling,
        )
    for c in range(4):
        keep_own(c).wait()
        drain(out.at[other, pl.ds(c * 4, 4)], last_recv.at[c])

    for c in range(4):
        drain(out.at[mine, pl.ds(c * 4, 4)], last_send.at[c])
    for c in range(2):
        drain(halves.at[other, pl.ds(c * 8, 8), core], half_send.at[c])
    tiles_sent(6)
    tiles_sent(7)
    drain(outgoing.at[most], back_send)
    drain(freq_mats.at[core, pl.ds(0, 3), 0], freq_send.at[0])
    drain(freq_mats.at[core, :, pl.ds(0, 3)], freq_send.at[1])
    drain(freq_mats.at[core], fpair_send)
    for m in range(2):
        drain(time_mats.at[m, pl.ds(0, 15), core, :, pl.ds(0, 256)], row_send.at[m])
        for side in range(2):
            drain(time_mats.at[m, :, core, :, pl.ds(0, 256)], side_send.at[m, side])
            drain(time_mats.at[m, pl.ds(0, 8), core, :, pl.ds(0, 256)], far_send.at[m, side])
        drain(time_mats.at[m, :, core], pair_send.at[m])


def place_kernel(parts, out, spread, store_sem):
    for h in range(2):
        def step(f, _, h=h):
            for k in range(8):
                spread[pl.ds(h * 16 * CELL + f * 8 + k, 16, stride=CELL), :] = parts[
                    k, f, pl.ds(h * 16, 16)
                ].astype(F32)
            return 0

        lax.fori_loop(0, 16, step, 0)

        def store(t, _):
            pltpu.make_async_copy(
                spread.at[pl.ds(pl.multiple_of(t * CELL, 8), 128)],
                out.at[pl.ds(pl.multiple_of(t * 128, 128), 128)],
                store_sem,
            ).start()
            return 0

        lax.fori_loop(h * 16, h * 16 + 16, store, 0)
    pltpu.make_async_copy(out, out, store_sem).wait()


def body(
    jones_gains, right_terms, normal_diagonal, normal_cross, station_flags,
    time_weights, time_kernel, channel_weights, channel_kernel,
):
    dma = pltpu.SemaphoreType.DMA
    scratch = [
        ((4096, 128), BF16), ((4096, 128), BF16), ((1024, 128), BF16), ((1024, 128), BF16),
        ((512, 64), jnp.int32), ((2, 32, 1024), BF16), ((2, 16, 256), BF16),
        ((32 * CELL, 128), F32), ((32 * CELL, 128), F32),
        ((32 * PAIR, 128), F32), ((32 * PAIR, 128), F32),
        ((32 * FLAG, 128), jnp.int32), ((8, 16, 2, 32, 128), BF16), ((CHIPS * TILE, 128), F32),
        ((4096, 128), BF16), ((4096, 128), BF16), ((512, 1024), BF16),
        ((2, 16, 2, 32, 1024), BF16), ((512, 1024), BF16), ((512, 1024), BF16),
        ((2, 4, 4, 16, 256), BF16), ((4096, 128), BF16), ((4096, 128), BF16),
        ((8, 16, 2, 32, 128), BF16),
    ]
    parts = pl.pallas_call(
        exchange_kernel,
        out_shape=jax.ShapeDtypeStruct((8, 16, 32, 128), BF16),
        in_specs=[pl.BlockSpec(memory_space=pltpu.HBM)] * 9,
        out_specs=pl.BlockSpec(memory_space=pltpu.VMEM),
        scratch_shapes=[
            *(pltpu.VMEM(shape, dtype) for shape, dtype in scratch),
            pltpu.SemaphoreType.REGULAR,
            pltpu.SemaphoreType.REGULAR,
            dma((9,)), dma((2,)), dma((2,)), dma((8,)), dma, dma((9,)),
            dma((2,)), dma((2,)), dma((2, 2)), dma((2, 2)), dma((2, 2)), dma((2, 2)),
            dma((2,)), dma((2,)),
            dma((2,)), dma((2,)), dma, dma, dma, dma, dma((4,)), dma((4,)),
        ],
        compiler_params=pltpu.CompilerParams(
            collective_id=0, has_side_effects=True, vmem_limit_bytes=56 * 1024 * 1024
        ),
    )(
        jones_gains.reshape(4096, 128),
        right_terms.reshape(4096, 128),
        normal_diagonal.reshape(1024, 128),
        normal_cross.reshape(1024, 128),
        station_flags.reshape(512, 64),
        time_weights, time_kernel, channel_weights, channel_kernel,
    )
    placed = pl.pallas_call(
        place_kernel,
        out_shape=jax.ShapeDtypeStruct((4096, 128), F32),
        in_specs=[pl.BlockSpec(memory_space=pltpu.VMEM)],
        out_specs=pl.BlockSpec(memory_space=pltpu.HBM),
        scratch_shapes=[pltpu.VMEM((32 * CELL, 128), F32), dma],
        compiler_params=pltpu.CompilerParams(vmem_limit_bytes=16 * 1024 * 1024),
    )(parts)
    return placed.reshape(32, 16, 8, 128)


def solution(mesh):
    cells = P("tm", "freq", None, None)
    in_specs = (
        cells, cells, cells, cells, P("tm", "freq", None),
        P("tm", None), P("tm", None), P("freq", None), P("freq", None),
    )
    return jax.shard_map(body, mesh=mesh, in_specs=in_specs, out_specs=cells, check_vma=False)
```

```python
import functools

import jax
import jax.numpy as jnp
from jax import lax
from jax.experimental import pallas as pl
from jax.experimental.pallas import tpu as pltpu
from jax.sharding import PartitionSpec as P

MESH = pl.DeviceIdType.MESH
BF16 = jnp.bfloat16
F32 = jnp.float32
SX, SY, SZ = 4, 8, 8
CHIPS = SX * SY * SZ
CELL, PAIR, FLAG, TILE = 136, 40, 24, 17
NT_DIMS = (((1,), (1,)), ((), ()))


def place():
    tm, freq = lax.axis_index("tm"), lax.axis_index("freq")
    return freq // 4, (freq % 4) * 2 + (tm // 2) % 2, tm // 4, tm % 2


def device(x, y, z, core):
    return (z * 4 + (y % 2) * 2 + core, x * 4 + y // 2)


def chip_slot(x, y, z):
    return (((x % 2) * 2 + x // 2) * SY + y) * SZ + z


def exchange_kernel(
    jones_in, right_in, diagonal_in, cross_in, flags_in, t_weights_in, t_kernel_in,
    f_weights_in, f_kernel_in,
    out,
    jones, right, diagonal, cross, flags, rows_own, freq_own,
    jones32, right32, diagonal32, cross32, flags_wide, halves, wide32, packed,
    arrived, columns, time_mats, mixed, smooth, freq_mats, outgoing,
    returned, parts,
    ready_y, ready_x, load_sem, half_send, half_recv, tile_send, tile_recv, own_sem,
    row_send, row_recv, side_send, side_recv, far_send, far_recv, pair_send, pair_recv,
    freq_send, freq_recv, fpair_send, fpair_recv, back_send, back_recv,
    last_send, last_recv,
):
    x, y, z, core = place()
    low, j = y % 2, x * 4 + y // 2
    block = z * 2 + low
    here = block * 16 + j
    me = chip_slot(x, y, z)
    sibling = device(x, y, z, 1 - core)
    mine, other = pl.ds(core * 4, 4), pl.ds((1 - core) * 4, 4)

    def on_x(k):
        return device((x + k) % SX, y, z, core)

    def on_y(k):
        return device(x, (y + k) % SY, z, core)

    def in_time(k):
        return device(x, y - low + (low + k) % 2, (z + k // 2) % SZ, core)

    def signal(semaphore, target):
        pl.semaphore_signal(semaphore, inc=1, device_id=target, device_id_type=MESH)

    def remote(src, dst, send, recv, target):
        pltpu.make_async_remote_copy(
            src_ref=src, dst_ref=dst, send_sem=send, recv_sem=recv,
            device_id=target, device_id_type=MESH,
        ).start()

    def drain(ref, semaphore):
        pltpu.make_async_copy(ref, ref, semaphore).wait()

    def tile(index):
        return pl.ds(pl.multiple_of(index * 16, 16), 16)

    barrier = pltpu.get_barrier_semaphore()
    signal(barrier, sibling)
    for k in range(1, 16):
        signal(barrier, in_time(k))
    for k in range(1, SY):
        @pl.when((y + k) % SY // 2 != y // 2)
        def _(k=k):
            signal(barrier, on_y(k))
    for k in range(1, SX):
        signal(barrier, on_x(k))

    loads = [
        pltpu.make_async_copy(src, dst, load_sem.at[n])
        for n, (src, dst) in enumerate(
            (
                (t_weights_in, rows_own.at[0]), (t_kernel_in, rows_own.at[1]),
                (f_weights_in, freq_own.at[0]), (f_kernel_in, freq_own.at[1]),
                (right_in, right), (jones_in, jones), (diagonal_in, diagonal),
                (cross_in, cross), (flags_in, flags),
            )
        )
    ]
    for load in loads:
        load.start()
    for load in loads[:4]:
        load.wait()
    pl.semaphore_wait(barrier, 1 + 15 + (SY - 2) + (SX - 1))
    for k in range(1, SY):
        signal(ready_y, on_y(k))

    quarter = pl.ds(pl.multiple_of(x * 256, 256), 256)

    def own_rows(m):
        return pltpu.make_async_copy(
            rows_own.at[m, :, quarter], time_mats.at[m, block, core, :, quarter], own_sem.at[m]
        )

    for m in range(2):
        own_rows(m).start()

        def send_rows(k, _, m=m):
            remote(
                rows_own.at[m, :, quarter], time_mats.at[m, block, core, :, quarter],
                row_send.at[m], row_recv.at[m], in_time(k),
            )
            return 0

        lax.fori_loop(1, 16, send_rows, 0)

    own_channels = freq_mats.at[core, x, y // 2]
    freq_mats[core, x, y // 2] = freq_own[core]
    for k in range(1, SX):
        remote(own_channels, own_channels, freq_send.at[0], freq_recv.at[0], on_x(k))

    for load in loads[4:]:
        load.wait()

    def spread(t, _):
        def move(src, dst, per, pitch):
            value = src[pl.ds(pl.multiple_of(t * per, per), per), :]
            dst[pl.ds(pl.multiple_of(t * pitch, 8), per), :] = value.astype(dst.dtype)

        move(jones, jones32, 128, CELL)
        move(right, right32, 128, CELL)
        move(diagonal, diagonal32, 32, PAIR)
        move(cross, cross32, 32, PAIR)
        flagged = flags[pl.ds(pl.multiple_of(t * 16, 16), 16), :]
        flags_wide[pl.ds(pl.multiple_of(t * FLAG, 8), 16), :] = jnp.concatenate(
            [flagged, flagged], axis=1
        )
        return 0

    lax.fori_loop(0, 32, spread, 0)

    def update(f, _):
        def part(ref, k, per, pitch):
            return ref[pl.ds(f * per + k, 32, stride=pitch), :]

        keep = part(flags_wide, 0, 1, FLAG) == 1
        upper, lower = part(diagonal32, 0, 2, PAIR), part(diagonal32, 1, 2, PAIR)
        real, imag = part(cross32, 0, 2, PAIR), part(cross32, 1, 2, PAIR)
        for offset in (0, 4):
            lead_r, lead_i, tail_r, tail_i = (
                part(right32, offset + k, 8, CELL) for k in range(4)
            )
            entries = (
                lead_r * upper + tail_r * real + tail_i * imag,
                lead_i * upper + tail_i * real - tail_r * imag,
                lead_r * real - lead_i * imag + tail_r * lower,
                lead_r * imag + lead_i * real + tail_i * lower,
            )
            for k, entry in enumerate(entries):
                previous = part(jones32, offset + k, 8, CELL)
                value = jnp.where(keep, previous, 0.5 * previous + 0.5 * entry)
                halves[offset + k, f, core] = value.astype(BF16)
        return 0

    def update_some(c):
        lax.fori_loop(c * 4, c * 4 + 4, update, 0)

    def send_half(c):
        some = halves.at[other, pl.ds(c * 8, 8), core]
        remote(some, some, half_send.at[c], half_recv.at[c], sibling)

    update_some(0)
    update_some(1)
    send_half(0)
    drain(freq_mats.at[core, pl.ds(0, 3), 0], freq_recv.at[0])
    column_channels = freq_mats.at[core, :, y // 2]
    for k in range(2, SY, 2):
        remote(column_channels, column_channels, freq_send.at[1], freq_recv.at[1], on_y(k))
    pl.semaphore_wait(ready_y, SY - 1)
    for k in range(1, SX):
        signal(ready_x, on_x(k))
    update_some(2)
    update_some(3)
    send_half(1)

    def send_sides(m):
        own_rows(m).wait()
        drain(time_mats.at[m, pl.ds(0, 15), core, :, pl.ds(0, 256)], row_recv.at[m])
        ref = time_mats.at[m, :, core, :, quarter]
        remote(ref, ref, side_send.at[m, 0], side_recv.at[m, 0], on_x(1))
        remote(ref, ref, side_send.at[m, 1], side_recv.at[m, 1], on_x(SX - 1))

    def quarter_of(k):
        return pl.ds(pl.multiple_of((x + k) % SX * 256, 256), 256)

    def forward_sides(m):
        ref = time_mats.at[m, pl.ds(0, 8), core, :, quarter_of(SX - 1)]
        drain(time_mats.at[m, :, core, :, quarter_of(SX - 1)], side_recv.at[m, 0])
        remote(ref, ref, far_send.at[m, 0], far_recv.at[m, 0], on_x(1))
        ref = time_mats.at[m, pl.ds(8, 8), core, :, quarter_of(1)]
        drain(time_mats.at[m, :, core, :, quarter_of(1)], side_recv.at[m, 1])
        remote(ref, ref, far_send.at[m, 1], far_recv.at[m, 1], on_x(SX - 1))

    def send_pair(m):
        for side in range(2):
            drain(time_mats.at[m, pl.ds(0, 8), core, :, quarter_of(2)], far_recv.at[m, side])
        ref = time_mats.at[m, :, core]
        remote(ref, ref, pair_send.at[m], pair_recv.at[m], sibling)

    def flip_pair(pair):
        def flip(f, _):
            stacked = jnp.concatenate(
                [
                    halves[core * 4 + pair * 2 + low, f].reshape(64, 128),
                    halves[core * 4 + pair * 2 + 1 - low, f].reshape(64, 128),
                ],
                axis=0,
            )
            wide32[pl.ds(pair * 128 * TILE + f, 128, stride=TILE), :] = stacked.T.astype(F32)
            return 0

        return flip

    def narrow_pair(pair):
        def narrow(step, _):
            for k in range(16):
                index = pair * 128 + step * 16 + k
                packed[tile(index), :] = wide32[pl.ds(index * TILE, 16), :].astype(BF16)
            return 0

        lax.fori_loop(0, 8, narrow, 0)

    def send_tiles(part):
        pair = odd if part < 4 else 1 - odd

        def send_tile(k, _):
            cx = (x // 2 + k // 64) % 2 * 2 + pair
            turn = k // 8 % 8
            cy, cz = (y + turn % 4 * 2 + turn // 4) % SY, (z + k) % SZ
            remote(
                packed.at[tile(chip_slot(cx, cy, cz))], arrived.at[tile(here)],
                tile_send.at[part], tile_recv, device(cx, cy, cz, core),
            )
            return 0

        start = part % 4 * 32
        lax.fori_loop(start + (part == 0), start + 32, send_tile, 0)

    def tiles_sent(part):
        drain(packed.at[pl.ds(0, 496 if part == 0 else 512)], tile_send.at[part])

    odd = x % 2
    for c in range(2):
        drain(halves.at[other, pl.ds(c * 8, 8), core], half_recv.at[c])
        lax.fori_loop(c * 8, c * 8 + 8, flip_pair(odd), 0)
    narrow_pair(odd)
    pl.semaphore_wait(ready_x, SX - 1)
    drain(freq_mats.at[core, :, pl.ds(0, 3)], freq_recv.at[1])
    remote(freq_mats.at[core], freq_mats.at[core], fpair_send, fpair_recv, sibling)
    own = pltpu.make_async_copy(packed.at[tile(me)], arrived.at[tile(here)], own_sem.at[3])
    own.start()
    send_sides(0)
    send_tiles(0)
    send_tiles(1)
    lax.fori_loop(0, 16, flip_pair(1 - odd), 0)
    narrow_pair(1 - odd)
    send_sides(1)
    tiles_sent(0)
    send_tiles(2)
    tiles_sent(1)
    send_tiles(3)
    tiles_sent(2)
    send_tiles(4)
    forward_sides(0)
    tiles_sent(3)
    send_tiles(5)
    forward_sides(1)
    tiles_sent(4)
    send_tiles(6)
    send_pair(0)
    tiles_sent(5)
    send_tiles(7)
    send_pair(1)
    drain(freq_mats.at[1 - core], fpair_recv)

    own.wait()
    most = pl.ds(0, (CHIPS - 1) * 16)
    drain(arrived.at[most], tile_recv)

    left = lax.broadcasted_iota(jnp.int32, (256, 128), 1) < 64

    def merge(step, _):
        first = arrived[pl.ds(pl.multiple_of(step * 512, 512), 256), :].astype(F32)
        second = arrived[pl.ds(pl.multiple_of(step * 512 + 256, 256), 256), :].astype(F32)
        lanes = pl.ds(pl.multiple_of(step * 128, 128), 128)
        columns[pl.ds(0, 256), lanes] = jnp.where(left, first, second).astype(BF16)
        columns[pl.ds(256, 256), lanes] = pltpu.roll(
            jnp.where(left, second, first), 64, 1
        ).astype(BF16)
        return 0

    lax.fori_loop(0, SZ, merge, 0)

    def times(m, source, n):
        matrix = time_mats[m, pl.ds(n * 4, 4)].reshape(256, 1024)
        return lax.dot_general(source[...], matrix, NT_DIMS, preferred_element_type=F32)

    drain(time_mats.at[0, :, 1 - core], pair_recv.at[0])

    for n in range(4):
        mixed[:, n * 256 : n * 256 + 256] = times(0, columns, n).astype(BF16)

    first_channels, second_channels = (freq_mats[m].reshape(256, 256) for m in range(2))

    for c in range(2):
        at = pl.ds(c * 256, 256)
        step = jnp.dot(first_channels, mixed[at, :], preferred_element_type=F32).astype(BF16)
        smooth[at, :] = jnp.dot(
            second_channels, step, preferred_element_type=F32
        ).astype(BF16)

    back = pltpu.make_async_copy(outgoing.at[tile(here)], returned.at[tile(me)], own_sem.at[4])
    drain(time_mats.at[1, :, 1 - core], pair_recv.at[1])

    def second_times(step, _):
        ahead = (3 - step) % 4
        pair = ((z + ahead) % SZ, (z + jnp.where(ahead == 0, 4, SZ - ahead)) % SZ)
        matrix = jnp.concatenate(
            [time_mats[1, pl.ds(cz * 2, 2)].reshape(128, 1024) for cz in pair], axis=0
        )
        result = lax.dot_general(smooth[...], matrix, NT_DIMS, preferred_element_type=F32)
        for half, cz in enumerate(pair):
            kept = result[:256, half * 128 : half * 128 + 128]
            turned = pltpu.roll(result[256:, half * 128 : half * 128 + 128], 64, 1)
            outgoing[pl.ds(pl.multiple_of(cz * 512, 512), 256), :] = jnp.where(
                left, kept, turned
            ).astype(BF16)
            outgoing[pl.ds(pl.multiple_of(cz * 512 + 256, 256), 256), :] = jnp.where(
                left, turned, kept
            ).astype(BF16)

        def send_back(k, _):
            cx, cy = (x + k // 16) % SX, (y + k // 2) % SY
            cz = jnp.where(k % 2 == 0, pair[0], pair[1])
            there = (cz * 2 + cy % 2) * 16 + cx * 4 + cy // 2

            @pl.when(there != here)
            def _():
                remote(
                    outgoing.at[tile(there)], returned.at[tile(me)],
                    back_send, back_recv, device(cx, cy, cz, core),
                )

            return 0

        lax.fori_loop(0, 64, send_back, 0)
        return 0

    lax.fori_loop(0, 4, second_times, 0)
    back.start()
    back.wait()
    drain(returned.at[most], back_recv)

    def rewiden(step, _):
        for k in range(16):
            index = step * 16 + k
            wide32[pl.ds(index * TILE, 16), :] = returned[tile(index), :].astype(F32)
        return 0

    lax.fori_loop(0, 16, rewiden, 0)

    def unflip(f, _):
        for pair in range(2):
            turned = wide32[pl.ds(pair * 128 * TILE + f, 128, stride=TILE), :].astype(BF16).T
            parts[core * 4 + pair * 2 + low, f] = turned[:64].reshape(2, 32, 128)
            parts[core * 4 + pair * 2 + 1 - low, f] = turned[64:].reshape(2, 32, 128)
        return 0

    def keep_own(c):
        some = pl.ds(c * 4, 4)
        return pltpu.make_async_copy(
            parts.at[mine, some, core], out.at[mine, some], own_sem.at[5 + c]
        )

    for c in range(4):
        lax.fori_loop(c * 4, c * 4 + 4, unflip, 0)
        keep_own(c).start()
        some = pl.ds(c * 4, 4)
        remote(
            parts.at[mine, some, 1 - core], out.at[mine, some],
            last_send.at[c], last_recv.at[c], sibling,
        )
    for c in range(4):
        keep_own(c).wait()
        drain(out.at[other, pl.ds(c * 4, 4)], last_recv.at[c])

    for c in range(4):
        drain(out.at[mine, pl.ds(c * 4, 4)], last_send.at[c])
    for c in range(2):
        drain(halves.at[other, pl.ds(c * 8, 8), core], half_send.at[c])
    tiles_sent(6)
    tiles_sent(7)
    drain(outgoing.at[most], back_send)
    drain(freq_mats.at[core, pl.ds(0, 3), 0], freq_send.at[0])
    drain(freq_mats.at[core, :, pl.ds(0, 3)], freq_send.at[1])
    drain(freq_mats.at[core], fpair_send)
    for m in range(2):
        drain(time_mats.at[m, pl.ds(0, 15), core, :, pl.ds(0, 256)], row_send.at[m])
        for side in range(2):
            drain(time_mats.at[m, :, core, :, pl.ds(0, 256)], side_send.at[m, side])
            drain(time_mats.at[m, pl.ds(0, 8), core, :, pl.ds(0, 256)], far_send.at[m, side])
        drain(time_mats.at[m, :, core], pair_send.at[m])


def place_kernel(parts, out, spread, store_sem):
    for h in range(2):
        def step(f, _, h=h):
            for k in range(8):
                spread[pl.ds(h * 16 * CELL + f * 8 + k, 16, stride=CELL), :] = parts[
                    k, f, pl.ds(h * 16, 16)
                ].astype(F32)
            return 0

        lax.fori_loop(0, 16, step, 0)

        def store(t, _):
            pltpu.make_async_copy(
                spread.at[pl.ds(pl.multiple_of(t * CELL, 8), 128)],
                out.at[pl.ds(pl.multiple_of(t * 128, 128), 128)],
                store_sem,
            ).start()
            return 0

        lax.fori_loop(h * 16, h * 16 + 16, store, 0)
    pltpu.make_async_copy(out, out, store_sem).wait()


def body(
    jones_gains, right_terms, normal_diagonal, normal_cross, station_flags,
    time_weights, time_kernel, channel_weights, channel_kernel,
):
    dma = pltpu.SemaphoreType.DMA
    scratch = [
        ((4096, 128), BF16), ((4096, 128), BF16), ((1024, 128), BF16), ((1024, 128), BF16),
        ((512, 64), jnp.int32), ((2, 32, 1024), BF16), ((2, 16, 256), BF16),
        ((32 * CELL, 128), F32), ((32 * CELL, 128), F32),
        ((32 * PAIR, 128), F32), ((32 * PAIR, 128), F32),
        ((32 * FLAG, 128), jnp.int32), ((8, 16, 2, 32, 128), BF16), ((CHIPS * TILE, 128), F32),
        ((4096, 128), BF16), ((4096, 128), BF16), ((512, 1024), BF16),
        ((2, 16, 2, 32, 1024), BF16), ((512, 1024), BF16), ((512, 1024), BF16),
        ((2, 4, 4, 16, 256), BF16), ((4096, 128), BF16), ((4096, 128), BF16),
        ((8, 16, 2, 32, 128), BF16),
    ]
    parts = pl.pallas_call(
        exchange_kernel,
        out_shape=jax.ShapeDtypeStruct((8, 16, 32, 128), BF16),
        in_specs=[pl.BlockSpec(memory_space=pltpu.HBM)] * 9,
        out_specs=pl.BlockSpec(memory_space=pltpu.VMEM),
        scratch_shapes=[
            *(pltpu.VMEM(shape, dtype) for shape, dtype in scratch),
            pltpu.SemaphoreType.REGULAR,
            pltpu.SemaphoreType.REGULAR,
            dma((9,)), dma((2,)), dma((2,)), dma((8,)), dma, dma((9,)),
            dma((2,)), dma((2,)), dma((2, 2)), dma((2, 2)), dma((2, 2)), dma((2, 2)),
            dma((2,)), dma((2,)),
            dma((2,)), dma((2,)), dma, dma, dma, dma, dma((4,)), dma((4,)),
        ],
        compiler_params=pltpu.CompilerParams(
            collective_id=0, has_side_effects=True, vmem_limit_bytes=56 * 1024 * 1024
        ),
    )(
        jones_gains.reshape(4096, 128),
        right_terms.reshape(4096, 128),
        normal_diagonal.reshape(1024, 128),
        normal_cross.reshape(1024, 128),
        station_flags.reshape(512, 64),
        time_weights, time_kernel, channel_weights, channel_kernel,
    )
    placed = pl.pallas_call(
        place_kernel,
        out_shape=jax.ShapeDtypeStruct((4096, 128), F32),
        in_specs=[pl.BlockSpec(memory_space=pltpu.VMEM)],
        out_specs=pl.BlockSpec(memory_space=pltpu.HBM),
        scratch_shapes=[pltpu.VMEM((32 * CELL, 128), F32), dma],
        compiler_params=pltpu.CompilerParams(vmem_limit_bytes=16 * 1024 * 1024),
    )(parts)
    return placed.reshape(32, 16, 8, 128)


def solution(mesh):
    cells = P("tm", "freq", None, None)
    in_specs = (
        cells, cells, cells, cells, P("tm", "freq", None),
        P("tm", None), P("tm", None), P("freq", None), P("freq", None),
    )
    return jax.shard_map(body, mesh=mesh, in_specs=in_specs, out_specs=cells, check_vma=False)
```
